128 devices in a mesh: box: 8 (over z, core), dir: 16 (over x, y).
Axes of the slice: x: 4, y: 4, z: 4, core: 2. Of those that a mesh axis runs over, the one named last changes fastest.
Arguments:
- currents: bfloat16 [16384, 256, 128], P(('box', 'dir')), may hold values from -6 to 6
- leaf_parent: int32 [16384], P(('box', 'dir')), may hold values from 0 to 255, as said below
- near_links: int32 [16384, 2], P(('box', 'dir')), may hold values 0 or 1
- near_blocks: bfloat16 [3, 256, 256], replicated, may hold values from -0.375 to 0.375
- aggregate_maps: bfloat16 [64, 256, 256], replicated, may hold values from -0.375 to 0.375
- far_boxes: int32 [256, 64], P('box'), may hold values from 0 to 255
- far_counts: int32 [256], P('box'), may hold values from 16 to 64
- translate_coef: float32 [256, 64, 256], P('box'), may hold values from 0.005 to 0.05
- time_kernel: float32 [128], replicated, may hold values from -0.5 to 0.5
- disaggregate_maps: bfloat16 [64, 256, 256], replicated, may hold values from -0.375 to 0.375
Outputs:
- field: bfloat16 [16384, 256, 128], P(('box', 'dir'))
The draws below stay inside these ranges and needn't reach their ends.
Inputs may be any that keep to these rules, and one draw needn't show every extreme that they name: `leaf_parent`: the leaves k * 64 to (k + 1) * 64 - 1 share one parent. The leaves g * 2048 to (g + 1) * 2048 - 1 have as parents the top-level boxes g * 32 to (g + 1) * 32 - 1, each exactly once as a run.
All inputs are finite; a program needn't handle non-finite values. No bound on the sum of `near_links` on one device may be relied on, other than what follows from the above.
Results may differ from the reference program's by a relative error of at most 0.0047.
Values may be sent and summed in bfloat16 or wider, within the bound.
No kernel may reach another device: no remote copies, remote signals or barrier semaphores. Data moves between devices by JAX's collectives and lax.ppermute only.
A program may use at most 192 MiB of HBM per device.

```python
import math
import jax
import jax.numpy as jnp
from jax import lax

P_SIZE = 256
K_TOP = 256
S = 128
LEAF_TOP = 64
FAR = 64
LEAVES = 16384
GROUP_LEAVES = 2048
TOP_DEV = 32
TOPS = 256


def draw_leaf_parent(key, part):
    group_count = LEAVES // GROUP_LEAVES
    group_keys = jax.random.split(jax.random.fold_in(key, 11), group_count)
    orders = jax.vmap(lambda k: jax.random.permutation(k, TOP_DEV))(group_keys).astype(jnp.int32)
    leaf_index = jnp.arange(LEAVES, dtype=jnp.int32)
    group = leaf_index // GROUP_LEAVES
    run_index = leaf_index % GROUP_LEAVES // LEAF_TOP
    return (group * TOP_DEV + orders[group, run_index]).astype(jnp.int32)


def set_ends(entries, key, low, high):
    spot = [jax.random.randint(jax.random.fold_in(key, axis), (), 0, length) for axis, length in enumerate(entries.shape)]
    widest = entries.shape.index(max(entries.shape))
    beside = spot[:widest] + [(spot[widest] + 1) % entries.shape[widest]] + spot[widest + 1:]
    return entries.at[tuple(spot)].set(low).at[tuple(beside)].set(high)


def level_of(stream_key, shape, shards, smallest, top_value):
    def one(axis_at, shards_of):
        draws = jax.random.uniform(jax.random.fold_in(jax.random.fold_in(stream_key, 6), axis_at), (shards_of,), jnp.float32, smallest / len(shards), top_value / len(shards))
        return jnp.repeat(jnp.exp(draws), shape[axis_at] // shards_of).reshape((-1,) + (1,) * (len(shape) - axis_at - 1))

    level = one(*shards[0])
    for cut in shards[1:]:
        level = level * one(*cut)
    return level


def bell_draw(own_key, dims, deviation, bound, cuts=(), kind=jnp.bfloat16):
    values = deviation * jax.random.normal(own_key, dims, jnp.float32)
    if cuts:
        values = values * level_of(own_key, dims, cuts, -0.22, 0.18)
    return jnp.clip(values, -bound, bound).astype(kind)


def setup_inputs(seed: int = 0) -> dict:
    key_of = jax.random.split(jax.random.key(seed), 11)
    currents = bell_draw(key_of[0], (LEAVES, P_SIZE, S), 1.0, 6.0, ((0, 128),))
    leaf_parent = draw_leaf_parent(jax.random.fold_in(key_of[10], 71), 0)
    near_links = set_ends((jax.random.randint(key_of[2], (LEAVES, 2), 0, 4) < 3).astype(jnp.int32), jax.random.fold_in(key_of[2], 1), 0, 1)
    near_blocks = bell_draw(key_of[3], (3, P_SIZE, P_SIZE), P_SIZE ** -0.5, 0.375)
    aggregate_maps = bell_draw(key_of[4], (LEAF_TOP, K_TOP, P_SIZE), P_SIZE ** -0.5, 0.375)
    far_boxes = set_ends(jax.random.randint(key_of[5], (TOPS, FAR), 0, TOPS), jax.random.fold_in(key_of[5], 1), 0, TOPS - 1).astype(jnp.int32)
    far_counts = set_ends(jax.random.randint(key_of[6], (TOPS,), FAR // 4, FAR + 1), jax.random.fold_in(key_of[6], 1), FAR // 4, FAR).astype(jnp.int32)
    translate_coef = jnp.clip(jnp.exp(math.log(0.05) - 2.3025851 * jax.random.uniform(key_of[7], (TOPS, FAR, K_TOP), jnp.float32) ** level_of(key_of[7], (TOPS, FAR, K_TOP), ((0, 8),), -0.2, 0.2)), 0.005, 0.05)
    time_kernel = bell_draw(key_of[8], (S,), S ** -0.5, 0.5, (), jnp.float32)
    disaggregate_maps = bell_draw(key_of[9], (LEAF_TOP, P_SIZE, K_TOP), K_TOP ** -0.5, 0.375)
    return dict(currents=currents, leaf_parent=leaf_parent, near_links=near_links, near_blocks=near_blocks, aggregate_maps=aggregate_maps, far_boxes=far_boxes, far_counts=far_counts, translate_coef=translate_coef, time_kernel=time_kernel, disaggregate_maps=disaggregate_maps)


def time_matrix(kernel):
    sample_lag = jnp.arange(S)[:, None] - jnp.arange(S)[None, :]
    return jnp.where(sample_lag >= 0, kernel[jnp.clip(sample_lag, 0, S - 1)], jnp.zeros((), kernel.dtype))


def reference(currents, leaf_parent, near_links, near_blocks, aggregate_maps, far_boxes, far_counts, translate_coef, time_kernel, disaggregate_maps):
    highest = lax.Precision.HIGHEST
    blocks = LEAVES // 8
    agg_float = aggregate_maps.astype(jnp.float32)
    cur_blocks = currents.reshape(blocks, 8, P_SIZE, S)
    par_blocks = leaf_parent.reshape(blocks, 8)
    block_ids = jnp.arange(blocks, dtype=jnp.int32)

    def add_block(running, inputs):
        block_cur, block_par, block_id = inputs
        first_map = ((block_id * 8) % LEAF_TOP).astype(jnp.int32)
        map_block = lax.dynamic_slice_in_dim(agg_float, first_map, 8, 0)
        ray_terms = jnp.einsum('sqp,spt->sqt', map_block, block_cur.astype(jnp.float32), precision=highest)
        return running.at[block_par].add(ray_terms), None

    top_rays, _ = lax.scan(add_block, jnp.zeros((TOPS, K_TOP, S), jnp.float32), (cur_blocks, par_blocks, block_ids))
    top_rays = top_rays.astype(jnp.bfloat16)
    is_valid = (jnp.arange(FAR)[None, :] < far_counts[:, None]).astype(jnp.float32)
    matches = (far_boxes[:, :, None] == jnp.arange(TOPS)[None, None, :]).astype(jnp.float32) * is_valid[:, :, None]
    weights = jnp.einsum('cfs,cfq->csq', matches, translate_coef, precision=highest)
    far_sum = jnp.einsum('csq,sqt->cqt', weights, top_rays.astype(jnp.float32), precision=highest)
    incoming = jnp.einsum('cqs,ts->cqt', far_sum, time_matrix(time_kernel), precision=highest).astype(jnp.bfloat16)
    incoming_float = incoming.astype(jnp.float32)
    zero_leaf = jnp.zeros((1, P_SIZE, S), currents.dtype)
    padded = jnp.concatenate([zero_leaf, currents, zero_leaf], axis=0)
    near_float = near_blocks.astype(jnp.float32)
    dis_float = disaggregate_maps.astype(jnp.float32)

    def leaf_block(block_index):
        first_leaf = (block_index * 8).astype(jnp.int32)
        first_map = (first_leaf % LEAF_TOP).astype(jnp.int32)
        before_leaf = lax.dynamic_slice_in_dim(padded, first_leaf, 8, 0).astype(jnp.float32)
        middle_leaf = lax.dynamic_slice_in_dim(padded, first_leaf + 1, 8, 0).astype(jnp.float32)
        after_leaf = lax.dynamic_slice_in_dim(padded, first_leaf + 2, 8, 0).astype(jnp.float32)
        link_mask = lax.dynamic_slice_in_dim(near_links, first_leaf, 8, 0).astype(jnp.float32)
        parents = lax.dynamic_slice_in_dim(leaf_parent, first_leaf, 8, 0)
        map_block = lax.dynamic_slice_in_dim(dis_float, first_map, 8, 0)
        near_field = jnp.einsum('pr,srt->spt', near_float[0], middle_leaf, precision=highest)
        near_field = near_field + link_mask[:, 0, None, None] * jnp.einsum('pr,srt->spt', near_float[1], before_leaf, precision=highest)
        near_field = near_field + link_mask[:, 1, None, None] * jnp.einsum('pr,srt->spt', near_float[2], after_leaf, precision=highest)
        far_field = jnp.einsum('spq,sqt->spt', map_block, incoming_float[parents], precision=highest)
        return (near_field + far_field).astype(jnp.bfloat16)

    field_out = lax.map(leaf_block, jnp.arange(blocks, dtype=jnp.int32))
    return field_out.reshape(LEAVES, P_SIZE, S)
```

```python
import jax
import jax.numpy as jnp
from jax import lax
from jax.experimental import pallas as pl
from jax.experimental.pallas import tpu as pltpu
from jax.sharding import PartitionSpec as P

AXES = ("box", "dir")
RUN = 64
SLOTS = 64
CHUNKS = 8
CHUNK = RUN // CHUNKS
UNK = 256
TIME = 128
DEVS = 128
ROWS = 8
F32, BF16 = jnp.float32, jnp.bfloat16
MIB = 1 << 20


def whole(space=pltpu.VMEM):
    return pl.BlockSpec(memory_space=space)


def params(mib):
    return pltpu.CompilerParams(vmem_limit_bytes=mib * MIB)


def aggregate(parent, counts, cur_hbm, agg_hbm, coef_hbm, boxes, cur, sent, maps, coef, wide, total, sems, coef_sems):
    cur_copies, map_copies = [], []
    for k in range(CHUNKS):
        for run in range(2):
            part = pl.ds(run * RUN + k * CHUNK, CHUNK)
            cur_copies.append(pltpu.make_async_copy(cur_hbm.at[part], cur.at[part], sems.at[run, k]))
        part = pl.ds(k * CHUNK, CHUNK)
        map_copies.append(pltpu.make_async_copy(agg_hbm.at[part], maps.at[part], sems.at[2, k]))
    own = [lax.rem(parent[run * RUN], boxes.shape[0]) for run in range(2)]
    coef_copies = [
        pltpu.make_async_copy(coef_hbm.at[own[run]], coef.at[run], coef_sems.at[run]) for run in range(2)
    ]
    for k in range(CHUNKS):
        cur_copies[2 * k].start()
        cur_copies[2 * k + 1].start()
        map_copies[k].start()
        if k == 0:
            for copy in coef_copies:
                copy.start()
    for copy in coef_copies:
        copy.wait()
    row = lax.broadcasted_iota(jnp.int32, (2 * SLOTS, UNK), 0)
    used = row < jnp.where(row < SLOTS, counts[own[0]], SLOTS + counts[own[1]])
    turned = jnp.where(used, coef[...].reshape(2 * SLOTS, UNK), 0.0).T
    for half in range(2):
        wide[pl.ds(4 + half, DEVS, stride=ROWS), :] = turned[half * DEVS : (half + 1) * DEVS]
    listed = jnp.concatenate([boxes[pl.ds(own[run], 1), :] for run in range(2)], axis=1)
    wide[pl.ds(6, DEVS, stride=ROWS), :] = jnp.broadcast_to(listed.astype(F32), (DEVS, 2 * SLOTS))
    lane = lax.broadcasted_iota(jnp.int32, (DEVS, 2 * SLOTS), 1)
    wide[pl.ds(7, DEVS, stride=ROWS), :] = jnp.where(lane < SLOTS, parent[0], parent[RUN]).astype(F32)

    for k in range(CHUNKS):
        cur_copies[2 * k].wait()
        cur_copies[2 * k + 1].wait()
        map_copies[k].wait()
        left = jnp.concatenate([maps[k * CHUNK + i] for i in range(CHUNK)], axis=1)
        right = jnp.concatenate(
            [cur[pl.ds(run * RUN + k * CHUNK, CHUNK)].reshape(CHUNK * UNK, TIME) for run in range(2)], axis=1
        )
        part = jnp.dot(left, right, preferred_element_type=F32)
        total[...] = part if k == 0 else total[...] + part
    for half in range(2):
        for run in range(2):
            wide[pl.ds(2 * half + run, DEVS, stride=ROWS), :] = total[
                half * DEVS : (half + 1) * DEVS, run * TIME : (run + 1) * TIME
            ]
    sent[...] = wide[...].astype(BF16)


def near(links, blocks, cur, low, high, dis_hbm, out, dis, sems):
    copies = [
        pltpu.make_async_copy(dis_hbm.at[pl.ds(k * CHUNK, CHUNK)], dis.at[pl.ds(k * CHUNK, CHUNK)], sems.at[k])
        for k in range(CHUNKS)
    ]
    for copy in copies:
        copy.start()
    left = jnp.concatenate([blocks[k] for k in range(3)], axis=1)

    def masked(leaf, side, value):
        return value * links[leaf, side].astype(F32).astype(BF16)

    def pair(i, before, after):
        own = jnp.concatenate([cur[i], cur[RUN + i]], axis=1)
        previous = jnp.concatenate(
            [masked(i, 0, before), masked(RUN + i, 0, cur[RUN + i - 1])], axis=1
        )
        following = jnp.concatenate([masked(i, 1, cur[i + 1]), masked(RUN + i, 1, after)], axis=1)
        right = jnp.concatenate([own, previous, following], axis=0)
        done = jnp.dot(left, right, preferred_element_type=F32)
        out[i] = done[:, :TIME]
        out[RUN + i] = done[:, TIME:]

    pair(0, low[...], cur[RUN + 1])

    @pl.loop(1, RUN - 1)
    def _(i):
        pair(i, cur[i - 1], cur[RUN + i + 1])

    pair(RUN - 1, cur[RUN - 2], high[...])
    for copy in copies:
        copy.wait()


def split(value):
    big = value.astype(BF16)
    return big, (value - big.astype(F32)).astype(BF16)


def translate(got, kernel, out, wide, tall):
    wide[...] = got[...].astype(F32)
    parents = wide[pl.ds(7, DEVS, stride=ROWS), :].T
    source = [parents[0:1], parents[SLOTS : SLOTS + 1]]
    coef = [wide[pl.ds(4 + half, DEVS, stride=ROWS), :] for half in range(2)]
    listed = wide[pl.ds(6, DEVS, stride=ROWS), :]
    lag = jnp.broadcast_to(kernel[...], (TIME, TIME))
    lag = pltpu.roll(lag, 0, 1, stride=1, stride_axis=0)
    row = lax.broadcasted_iota(jnp.int32, (TIME, TIME), 0)
    column = lax.broadcasted_iota(jnp.int32, (TIME, TIME), 1)
    lag_big, lag_rest = split(jnp.where(column >= row, lag, 0.0))
    rows = []
    for run in range(2):
        for block in range(DEVS // 8):
            at = slice(block * 8, block * 8 + 8)
            weight = [[jnp.zeros((8, DEVS), F32) for _ in range(2)] for _ in range(2)]
            for slot in range(run * SLOTS, (run + 1) * SLOTS):
                name = listed[at, slot : slot + 1]
                for side in range(2):
                    here = name == source[side]
                    for half in range(2):
                        weight[half][side] = weight[half][side] + jnp.where(
                            here, coef[half][at, slot : slot + 1], 0.0
                        )
            rows.append([jnp.concatenate(weight[half], axis=1) for half in range(2)])
    for half in range(2):
        rays = jnp.concatenate(
            [wide[pl.ds(2 * half + run, DEVS, stride=ROWS), :] for run in range(2)], axis=0
        ).astype(BF16)
        big, rest = split(jnp.concatenate([r[half] for r in rows], axis=0))
        far = jnp.dot(big, rays, preferred_element_type=F32) + jnp.dot(rest, rays, preferred_element_type=F32)
        far_big, far_rest = split(far)
        done = (
            jnp.dot(far_big, lag_big, preferred_element_type=F32)
            + jnp.dot(far_rest, lag_big, preferred_element_type=F32)
            + jnp.dot(far_big, lag_rest, preferred_element_type=F32)
        )
        for run in range(2):
            tall[pl.ds(2 * half + run, DEVS, stride=4), :] = done[run * DEVS : (run + 1) * DEVS]
    out[...] = tall[...].astype(BF16)


def disaggregate(got, near_field, dis, out, tall, incoming):
    step = pl.program_id(0)

    @pl.when(step == 0)
    def _():
        tall[...] = got[...].astype(F32)
        for half in range(2):
            for run in range(2):
                incoming[half * DEVS : (half + 1) * DEVS, run * TIME : (run + 1) * TIME] = tall[
                    pl.ds(2 * half + run, DEVS, stride=4), :
                ].astype(BF16)

    for i in range(CHUNK):
        leaf = step * CHUNK + i
        far = jnp.dot(dis[leaf], incoming[...], preferred_element_type=F32)
        for run in range(2):
            out[run, i] = (near_field[run * RUN + leaf] + far[:, run * TIME : (run + 1) * TIME]).astype(BF16)


def per_device(
    currents,
    leaf_parent,
    near_links,
    near_blocks,
    aggregate_maps,
    far_boxes,
    far_counts,
    translate_coef,
    time_kernel,
    disaggregate_maps,
):
    leaves = 2 * RUN
    low = lax.ppermute(currents[leaves - 1], AXES, [(i, i + 1) for i in range(DEVS - 1)])
    high = lax.ppermute(currents[0], AXES, [(i + 1, i) for i in range(DEVS - 1)])
    held, sent = pl.pallas_call(
        aggregate,
        out_shape=(
            pltpu.VMEM((leaves, UNK, TIME), BF16),
            jax.ShapeDtypeStruct((DEVS * ROWS, TIME), BF16),
        ),
        in_specs=[
            whole(pltpu.SMEM),
            whole(pltpu.SMEM),
            whole(pl.ANY),
            whole(pl.ANY),
            whole(pl.ANY),
            whole(),
        ],
        out_specs=(whole(), whole()),
        scratch_shapes=[
            pltpu.VMEM((RUN, UNK, UNK), BF16),
            pltpu.VMEM((2, SLOTS, UNK), F32),
            pltpu.VMEM((DEVS * ROWS, TIME), F32),
            pltpu.VMEM((UNK, UNK), F32),
            pltpu.SemaphoreType.DMA((3, CHUNKS)),
            pltpu.SemaphoreType.DMA((2,)),
        ],
        compiler_params=params(20),
        cost_estimate=pl.CostEstimate(flops=2 << 30, bytes_accessed=17 * MIB, transcendentals=0),
        name="aggregate",
    )(leaf_parent, far_counts, currents, aggregate_maps, translate_coef, far_boxes)
    arrived = lax.all_to_all(sent.reshape(DEVS, ROWS, TIME), AXES, 0, 0, tiled=True)
    near_field, dis = pl.pallas_call(
        near,
        out_shape=(
            pltpu.VMEM((leaves, UNK, TIME), F32),
            pltpu.VMEM((RUN, UNK, UNK), BF16),
        ),
        in_specs=[whole(pltpu.SMEM), whole(), whole(), whole(), whole(), whole(pl.ANY)],
        out_specs=(whole(), whole()),
        scratch_shapes=[pltpu.SemaphoreType.DMA((CHUNKS,))],
        compiler_params=params(12),
        cost_estimate=pl.CostEstimate(flops=6 << 30, bytes_accessed=17 * MIB, transcendentals=0),
        name="near",
    )(
        near_links,
        near_blocks,
        pltpu.with_memory_space_constraint(held, pltpu.VMEM),
        low,
        high,
        disaggregate_maps,
    )
    incoming = pl.pallas_call(
        translate,
        out_shape=jax.ShapeDtypeStruct((DEVS * 4, TIME), BF16),
        in_specs=[whole(), whole()],
        out_specs=whole(),
        scratch_shapes=[pltpu.VMEM((DEVS * ROWS, TIME), F32), pltpu.VMEM((DEVS * 4, TIME), F32)],
        compiler_params=params(12),
        cost_estimate=pl.CostEstimate(flops=1 << 28, bytes_accessed=MIB, transcendentals=0),
        name="translate",
    )(arrived.reshape(DEVS * ROWS, TIME), time_kernel.reshape(1, TIME))
    returned = lax.all_to_all(incoming.reshape(DEVS, 4, TIME), AXES, 0, 0, tiled=True)
    field = pl.pallas_call(
        disaggregate,
        grid=(CHUNKS,),
        out_shape=jax.ShapeDtypeStruct((2, RUN, UNK, TIME), BF16),
        in_specs=[whole(), whole(), whole()],
        out_specs=pl.BlockSpec((2, CHUNK, UNK, TIME), lambda i: (0, i, 0, 0)),
        scratch_shapes=[pltpu.VMEM((DEVS * 4, TIME), F32), pltpu.VMEM((UNK, UNK), BF16)],
        compiler_params=params(12),
        cost_estimate=pl.CostEstimate(flops=2 << 30, bytes_accessed=9 * MIB, transcendentals=0),
        name="disaggregate",
    )(
        returned.reshape(DEVS * 4, TIME),
        pltpu.with_memory_space_constraint(near_field, pltpu.VMEM),
        pltpu.with_memory_space_constraint(dis, pltpu.VMEM),
    )
    return field.reshape(leaves, UNK, TIME)


def solution(mesh):
    in_specs = (
        P(AXES, None, None),
        P(AXES),
        P(AXES, None),
        P(),
        P(),
        P("box", None),
        P("box"),
        P("box", None, None),
        P(),
        P(),
    )
    return jax.shard_map(
        per_device, mesh=mesh, in_specs=in_specs, out_specs=P(AXES, None, None), check_vma=False
    )
```

```python
import jax
import jax.numpy as jnp
from jax import lax
from jax.experimental import pallas as pl
from jax.experimental.pallas import tpu as pltpu
from jax.sharding import PartitionSpec as P

AXES = ("box", "dir")
RUN = 64
SLOTS = 64
CHUNKS = 8
CHUNK = RUN // CHUNKS
EARLY = 32
EDGE = (RUN - EARLY) // 2
STEP = 8
AHEAD = 3
UNK = 256
TIME = 128
DEVS = 128
ROWS = 16
F32, BF16 = jnp.float32, jnp.bfloat16
NEAR = BF16
MIB = 1 << 20


def whole(space=pltpu.VMEM):
    return pl.BlockSpec(memory_space=space)


def params(mib):
    return pltpu.CompilerParams(vmem_limit_bytes=mib * MIB)


def in_hbm(*arrays):
    return [pltpu.with_memory_space_constraint(array, pltpu.HBM) for array in arrays]


def split(value):
    big = value.astype(BF16)
    return big, (value - big.astype(F32)).astype(BF16)


def aggregate(
    parent_hbm, counts_hbm, boxes_hbm, coef_hbm, cur_hbm, agg_hbm, sent,
    cur, maps, coef, boxes, parent, counts, wide, total, sems, small_sems,
):
    small = [
        pltpu.make_async_copy(source, target, small_sems.at[k])
        for k, (source, target) in enumerate(
            ((parent_hbm, parent), (counts_hbm, counts), (boxes_hbm, boxes))
        )
    ]
    for copy in small:
        copy.start()
    big = []
    for k in range(CHUNKS):
        part = pl.ds(k * CHUNK, CHUNK)
        second = pl.ds(RUN + k * CHUNK, CHUNK)
        big.append(
            (
                pltpu.make_async_copy(cur_hbm.at[part], cur.at[part], sems.at[0, k]),
                pltpu.make_async_copy(cur_hbm.at[second], cur.at[second], sems.at[1, k]),
                pltpu.make_async_copy(agg_hbm.at[part], maps.at[part], sems.at[2, k]),
            )
        )
    for copies in big[:AHEAD]:
        for copy in copies:
            copy.start()
    for copy in small:
        copy.wait()
    own = [lax.rem(parent[run * RUN], boxes.shape[0]) for run in range(2)]
    coef_copies = [
        pltpu.make_async_copy(coef_hbm.at[own[run]], coef.at[run], small_sems.at[3 + run]) for run in range(2)
    ]
    for copy in coef_copies:
        copy.start()

    def rays(k):
        for copy in big[k]:
            copy.wait()
        for copies in big[k + AHEAD : k + AHEAD + 1]:
            for copy in copies:
                copy.start()
        left = jnp.concatenate([maps[k * CHUNK + i] for i in range(CHUNK)], axis=1)
        right = jnp.concatenate(
            [cur[pl.ds(run * RUN + k * CHUNK, CHUNK)].reshape(CHUNK * UNK, TIME) for run in range(2)], axis=1
        )
        return jnp.dot(left, right, preferred_element_type=F32)

    total[...] = rays(0)
    for k in range(1, CHUNKS // 2):
        total[...] = total[...] + rays(k)
    for copy in coef_copies:
        copy.wait()
    row = lax.broadcasted_iota(jnp.int32, (2 * SLOTS, UNK), 0)
    used = row < jnp.where(row < SLOTS, counts[own[0]], SLOTS + counts[own[1]])
    turned = jnp.where(used, coef[...].reshape(2 * SLOTS, UNK), 0.0).T
    listed = jnp.concatenate([boxes[pl.ds(own[run], 1), :] for run in range(2)], axis=1)
    listed = jnp.broadcast_to(listed.astype(F32), (2 * SLOTS, 2 * SLOTS)).T[:, :1]
    lane = lax.broadcasted_iota(jnp.int32, (2 * SLOTS, 2 * DEVS), 1).astype(F32)
    match = jnp.where(listed == lane, 1.0, 0.0).astype(BF16)
    coef_big, coef_rest = split(turned)
    for run in range(2):
        at = slice(run * SLOTS, (run + 1) * SLOTS)
        weight = jnp.dot(coef_big[:, at], match[at], preferred_element_type=F32) + jnp.dot(
            coef_rest[:, at], match[at], preferred_element_type=F32
        )
        for half in range(2):
            for side in range(2):
                wide[pl.ds(4 + half * 4 + run * 2 + side, DEVS, stride=ROWS), :] = weight[
                    half * DEVS : (half + 1) * DEVS, side * DEVS : (side + 1) * DEVS
                ]
    lane = lax.broadcasted_iota(jnp.int32, (DEVS, TIME), 1)
    wide[pl.ds(12, DEVS, stride=ROWS), :] = jnp.where(lane < RUN, parent[0], parent[RUN]).astype(F32)
    for spare in range(13, ROWS):
        wide[pl.ds(spare, DEVS, stride=ROWS), :] = jnp.zeros((DEVS, TIME), F32)
    for k in range(CHUNKS // 2, CHUNKS):
        total[...] = total[...] + rays(k)
    for half in range(2):
        for run in range(2):
            wide[pl.ds(2 * half + run, DEVS, stride=ROWS), :] = total[
                half * DEVS : (half + 1) * DEVS, run * TIME : (run + 1) * TIME
            ]
    sent[...] = wide[...].astype(BF16)


def around(links, cur, leaf, at):
    def linked(run, side):
        value = cur[run, at + 2 * side - 1]
        return value * links[run * RUN + leaf, side].astype(F32).astype(BF16)

    own = jnp.concatenate([cur[run, at] for run in range(2)], axis=1)
    return [own] + [jnp.concatenate([linked(run, side) for run in range(2)], axis=1) for side in range(2)]


def near(links, cur_hbm, blocks_hbm, out_hbm, cur, blocks, stage, in_sems, blocks_sem, out_sems):
    steps = EARLY // STEP

    def fetch(k, run):
        first = 0 if k == 0 else 2 + k * STEP
        count = 2 + (k + 1) * STEP - first
        return pltpu.make_async_copy(
            cur_hbm.at[pl.ds(run * RUN + EDGE - 1 + first, count)],
            cur.at[run, pl.ds(first, count)],
            in_sems.at[run, k],
        )

    def store(k, run):
        return pltpu.make_async_copy(
            stage.at[run, pl.ds(k * STEP, STEP)], out_hbm.at[run, pl.ds(k * STEP, STEP)], out_sems.at[run, k]
        )

    load = pltpu.make_async_copy(blocks_hbm, blocks, blocks_sem)
    load.start()
    for k in range(steps):
        for run in range(2):
            fetch(k, run).start()
    load.wait()
    left = jnp.concatenate([blocks[j] for j in range(3)], axis=1)
    for k in range(steps):
        for run in range(2):
            fetch(k, run).wait()
        for j in range(k * STEP, (k + 1) * STEP):
            right = jnp.concatenate(around(links, cur, EDGE + j, 1 + j), axis=0)
            done = jnp.dot(left, right, preferred_element_type=F32)
            for run in range(2):
                stage[run, j] = done[:, run * TIME : (run + 1) * TIME].astype(NEAR)
        for run in range(2):
            store(k, run).start()
    for k in range(steps):
        for run in range(2):
            store(k, run).wait()


def translate(got, kernel, out, wide, tall):
    wide[...] = got[...].astype(F32)
    parents = wide[pl.ds(12, DEVS, stride=ROWS), :].T
    source = jnp.concatenate([parents[0:1], parents[RUN : RUN + 1]], axis=1)
    box = lax.broadcasted_iota(jnp.int32, (2 * DEVS, 2 * DEVS), 0).astype(F32)
    place = jnp.where(box == source, 1.0, 0.0).astype(BF16)
    rays = jnp.concatenate(
        [
            jnp.concatenate([wide[pl.ds(2 * half + run, DEVS, stride=ROWS), :] for half in range(2)], axis=1)
            for run in range(2)
        ],
        axis=0,
    )
    rays = jnp.dot(place, rays.astype(BF16), preferred_element_type=F32).astype(BF16)
    lag = jnp.broadcast_to(kernel[...], (TIME, TIME))
    lag = pltpu.roll(lag, 0, 1, stride=1, stride_axis=0)
    row = lax.broadcasted_iota(jnp.int32, (TIME, TIME), 0)
    column = lax.broadcasted_iota(jnp.int32, (TIME, TIME), 1)
    lag_big, lag_rest = split(jnp.where(column >= row, lag, 0.0))
    far = []
    for half in range(2):
        weight = jnp.concatenate(
            [
                jnp.concatenate(
                    [wide[pl.ds(4 + half * 4 + run * 2 + side, DEVS, stride=ROWS), :] for side in range(2)], axis=1
                )
                for run in range(2)
            ],
            axis=0,
        )
        far.append(
            jnp.dot(weight.astype(BF16), rays[:, half * TIME : (half + 1) * TIME], preferred_element_type=F32)
        )
    big, rest = split(jnp.concatenate(far, axis=0))
    done = (
        jnp.dot(big, lag_big, preferred_element_type=F32)
        + jnp.dot(rest, lag_big, preferred_element_type=F32)
        + jnp.dot(big, lag_rest, preferred_element_type=F32)
    )
    for k in range(4):
        tall[pl.ds(k, DEVS, stride=4), :] = done[k * DEVS : (k + 1) * DEVS]
    out[...] = tall[...].astype(BF16)


def disaggregate(
    links, got, low, high, blocks_hbm, cur_hbm, near_hbm, dis_hbm, out_hbm,
    blocks, cur, early, dis, stage, tall, incoming, cur_sems, early_sems, side_sems, out_sems,
):
    late = [(k % 2 * (RUN - EDGE) + k // 2 * STEP) for k in range(2 * EDGE // STEP)]
    early_steps = [EDGE + k * STEP for k in range(EARLY // STEP)]
    order = []
    for k in range(max(len(late), len(early_steps))):
        order += [(k, late[k], True)] if k < len(late) else []
        order += [(k, early_steps[k], False)] if k < len(early_steps) else []

    def fetch(k, first, is_late):
        at = pl.ds(first, STEP)
        copies = [pltpu.make_async_copy(dis_hbm.at[at], dis.at[at], side_sems.at[first // STEP])]
        for run in range(2):
            if is_late:
                start, end = first - 1, first + STEP + 1
                start = max(start, 0) if run == 0 else start
                end = min(end, RUN) if run == 1 else end
                copies.append(
                    pltpu.make_async_copy(
                        cur_hbm.at[pl.ds(run * RUN + start, end - start)],
                        cur.at[k, run, pl.ds(start - first + 1, end - start)],
                        cur_sems.at[run, k],
                    )
                )
            else:
                part = pl.ds(k * STEP, STEP)
                copies.append(
                    pltpu.make_async_copy(near_hbm.at[run, part], early.at[run, part], early_sems.at[run, k])
                )
        return copies

    def store(first, run):
        at = pl.ds(run * RUN + first, STEP)
        return pltpu.make_async_copy(stage.at[at], out_hbm.at[at], out_sems.at[run, first // STEP])

    load = pltpu.make_async_copy(blocks_hbm, blocks, side_sems.at[RUN // STEP])
    load.start()
    for part in order:
        for copy in fetch(*part):
            copy.start()
    cur[late.index(0), 0, 0] = low[...]
    cur[late.index(RUN - STEP), 1, STEP + 1] = high[...]
    tall[...] = got[...].astype(F32)
    for half in range(2):
        for run in range(2):
            incoming[half * DEVS : (half + 1) * DEVS, run * TIME : (run + 1) * TIME] = tall[
                pl.ds(2 * half + run, DEVS, stride=4), :
            ].astype(BF16)
    load.wait()
    left = jnp.concatenate([blocks[j] for j in range(3)], axis=1)
    for part in order:
        for copy in fetch(*part):
            copy.wait()
        k, first, is_late = part
        for j in range(STEP):
            leaf = first + j
            if is_late:
                right = jnp.concatenate(around(links, cur.at[k], leaf, 1 + j) + [incoming[...]], axis=0)
                done = jnp.dot(jnp.concatenate([left, dis[leaf]], axis=1), right, preferred_element_type=F32)
            else:
                done = jnp.dot(dis[leaf], incoming[...], preferred_element_type=F32)
            for run in range(2):
                value = done[:, run * TIME : (run + 1) * TIME]
                if not is_late:
                    value = value + early[run, k * STEP + j].astype(F32)
                stage[run * RUN + leaf] = value.astype(BF16)
        for run in range(2):
            store(first, run).start()
    for part in order:
        for run in range(2):
            store(part[1], run).wait()


def per_device(
    currents,
    leaf_parent,
    near_links,
    near_blocks,
    aggregate_maps,
    far_boxes,
    far_counts,
    translate_coef,
    time_kernel,
    disaggregate_maps,
):
    leaves = 2 * RUN
    hbm = whole(pltpu.HBM)
    first, last = currents[0], currents[leaves - 1]
    sent = pl.pallas_call(
        aggregate,
        out_shape=jax.ShapeDtypeStruct((DEVS * ROWS, TIME), BF16),
        in_specs=[hbm] * 6,
        out_specs=whole(),
        scratch_shapes=[
            pltpu.VMEM((leaves, UNK, TIME), BF16),
            pltpu.VMEM((RUN, UNK, UNK), BF16),
            pltpu.VMEM((2, SLOTS, UNK), F32),
            pltpu.VMEM(far_boxes.shape, jnp.int32),
            pltpu.SMEM(leaf_parent.shape, jnp.int32),
            pltpu.SMEM(far_counts.shape, jnp.int32),
            pltpu.VMEM((DEVS * ROWS, TIME), F32),
            pltpu.VMEM((UNK, UNK), F32),
            pltpu.SemaphoreType.DMA((3, CHUNKS)),
            pltpu.SemaphoreType.DMA((5,)),
        ],
        compiler_params=params(40),
        cost_estimate=pl.CostEstimate(flops=2 << 30, bytes_accessed=17 * MIB, transcendentals=0),
        name="aggregate",
    )(*in_hbm(leaf_parent, far_counts, far_boxes, translate_coef, currents, aggregate_maps))
    arrived = lax.all_to_all(sent.reshape(DEVS, ROWS, TIME), AXES, 0, 0, tiled=True)
    early = pl.pallas_call(
        near,
        out_shape=pltpu.HBM((2, EARLY, UNK, TIME), NEAR),
        in_specs=[whole(pltpu.SMEM)] + [hbm] * 2,
        out_specs=hbm,
        scratch_shapes=[
            pltpu.VMEM((2, EARLY + 2, UNK, TIME), BF16),
            pltpu.VMEM((3, UNK, UNK), BF16),
            pltpu.VMEM((2, EARLY, UNK, TIME), NEAR),
            pltpu.SemaphoreType.DMA((2, EARLY // STEP)),
            pltpu.SemaphoreType.DMA(()),
            pltpu.SemaphoreType.DMA((2, EARLY // STEP)),
        ],
        compiler_params=params(40),
        cost_estimate=pl.CostEstimate(flops=3 << 30, bytes_accessed=12 * MIB, transcendentals=0),
        name="near",
    )(near_links, *in_hbm(currents, near_blocks))
    arrived, early, first, last = lax.optimization_barrier((arrived, early, first, last))
    incoming = pl.pallas_call(
        translate,
        out_shape=jax.ShapeDtypeStruct((DEVS * 4, TIME), BF16),
        in_specs=[whole(), whole()],
        out_specs=whole(),
        scratch_shapes=[pltpu.VMEM((DEVS * ROWS, TIME), F32), pltpu.VMEM((DEVS * 4, TIME), F32)],
        compiler_params=params(12),
        cost_estimate=pl.CostEstimate(flops=1 << 28, bytes_accessed=MIB, transcendentals=0),
        name="translate",
    )(arrived.reshape(DEVS * ROWS, TIME), time_kernel.reshape(1, TIME))
    incoming, first, last = lax.optimization_barrier((incoming, first, last))
    returned = lax.all_to_all(incoming.reshape(DEVS, 4, TIME), AXES, 0, 0, tiled=True)
    low = lax.ppermute(last, AXES, [(i, i + 1) for i in range(DEVS - 1)])
    high = lax.ppermute(first, AXES, [(i + 1, i) for i in range(DEVS - 1)])
    return pl.pallas_call(
        disaggregate,
        out_shape=pltpu.HBM((leaves, UNK, TIME), BF16),
        in_specs=[whole(pltpu.SMEM)] + [whole()] * 3 + [hbm] * 4,
        out_specs=hbm,
        scratch_shapes=[
            pltpu.VMEM((3, UNK, UNK), BF16),
            pltpu.VMEM((2 * EDGE // STEP, 2, STEP + 2, UNK, TIME), BF16),
            pltpu.VMEM((2, EARLY, UNK, TIME), NEAR),
            pltpu.VMEM((RUN, UNK, UNK), BF16),
            pltpu.VMEM((leaves, UNK, TIME), BF16),
            pltpu.VMEM((DEVS * 4, TIME), F32),
            pltpu.VMEM((UNK, UNK), BF16),
            pltpu.SemaphoreType.DMA((2, 2 * EDGE // STEP)),
            pltpu.SemaphoreType.DMA((2, EARLY // STEP)),
            pltpu.SemaphoreType.DMA((RUN // STEP + 1,)),
            pltpu.SemaphoreType.DMA((2, RUN // STEP)),
        ],
        compiler_params=params(50),
        cost_estimate=pl.CostEstimate(flops=5 << 30, bytes_accessed=28 * MIB, transcendentals=0),
        name="disaggregate",
    )(
        near_links,
        returned.reshape(DEVS * 4, TIME),
        low,
        high,
        *in_hbm(near_blocks, currents, early, disaggregate_maps),
    )


def solution(mesh):
    in_specs = (
        P(AXES, None, None),
        P(AXES),
        P(AXES, None),
        P(),
        P(),
        P("box", None),
        P("box"),
        P("box", None, None),
        P(),
        P(),
    )
    return jax.shard_map(
        per_device, mesh=mesh, in_specs=in_specs, out_specs=P(AXES, None, None), check_vma=False
    )
```

```python
import jax
import jax.numpy as jnp
from jax import lax
from jax.experimental import pallas as pl
from jax.experimental.pallas import tpu as pltpu
from jax.sharding import PartitionSpec as P

AXES = ("box", "dir")
RUN = 64
SLOTS = 64
CHUNKS = 8
CHUNK = RUN // CHUNKS
EARLY = 32
EDGE = (RUN - EARLY) // 2
STEP = 8
AHEAD = 3
UNK = 256
TIME = 128
DEVS = 128
ROWS = 16
F32, BF16 = jnp.float32, jnp.bfloat16
BACK = 8
NO_WEIGHT = 2.0**-30
NEAR = BF16
MIB = 1 << 20


def whole(space=pltpu.VMEM):
    return pl.BlockSpec(memory_space=space)


def params(mib):
    return pltpu.CompilerParams(vmem_limit_bytes=mib * MIB)


def in_hbm(*arrays):
    return [pltpu.with_memory_space_constraint(array, pltpu.HBM) for array in arrays]


def split(value):
    big = value.astype(BF16)
    return big, (value - big.astype(F32)).astype(BF16)


def aggregate(
    parent_hbm, counts_hbm, boxes_hbm, coef_hbm, cur_hbm, agg_hbm, sent,
    cur, maps, coef, boxes, parent, counts, wide, total, sems, small_sems,
):
    small = [
        pltpu.make_async_copy(source, target, small_sems.at[k])
        for k, (source, target) in enumerate(
            ((parent_hbm, parent), (counts_hbm, counts), (boxes_hbm, boxes))
        )
    ]
    for copy in small:
        copy.start()
    big = []
    for k in range(CHUNKS):
        part = pl.ds(k * CHUNK, CHUNK)
        second = pl.ds(RUN + k * CHUNK, CHUNK)
        big.append(
            (
                pltpu.make_async_copy(cur_hbm.at[part], cur.at[part], sems.at[0, k]),
                pltpu.make_async_copy(cur_hbm.at[second], cur.at[second], sems.at[1, k]),
                pltpu.make_async_copy(agg_hbm.at[part], maps.at[part], sems.at[2, k]),
            )
        )
    for copies in big[:AHEAD]:
        for copy in copies:
            copy.start()
    for copy in small:
        copy.wait()
    own = [lax.rem(parent[run * RUN], boxes.shape[0]) for run in range(2)]
    coef_copies = [
        pltpu.make_async_copy(coef_hbm.at[own[run]], coef.at[run], small_sems.at[3 + run]) for run in range(2)
    ]
    for copy in coef_copies:
        copy.start()

    def rays(k):
        for copy in big[k]:
            copy.wait()
        for copies in big[k + AHEAD : k + AHEAD + 1]:
            for copy in copies:
                copy.start()
        left = jnp.concatenate([maps[k * CHUNK + i] for i in range(CHUNK)], axis=1)
        right = jnp.concatenate(
            [cur[pl.ds(run * RUN + k * CHUNK, CHUNK)].reshape(CHUNK * UNK, TIME) for run in range(2)], axis=1
        )
        return jnp.dot(left, right, preferred_element_type=F32)

    total[...] = rays(0)
    for k in range(1, CHUNKS // 2):
        total[...] = total[...] + rays(k)
    for copy in coef_copies:
        copy.wait()
    row = lax.broadcasted_iota(jnp.int32, (2 * SLOTS, UNK), 0)
    used = row < jnp.where(row < SLOTS, counts[own[0]], SLOTS + counts[own[1]])
    turned = jnp.where(used, coef[...].reshape(2 * SLOTS, UNK), 0.0).T
    listed = jnp.concatenate([boxes[pl.ds(own[run], 1), :] for run in range(2)], axis=1)
    listed = jnp.broadcast_to(listed.astype(F32), (2 * SLOTS, 2 * SLOTS)).T[:, :1]
    lane = lax.broadcasted_iota(jnp.int32, (2 * SLOTS, 2 * DEVS), 1).astype(F32)
    match = jnp.where(listed == lane, 1.0, 0.0).astype(BF16)
    coef_big, coef_rest = split(turned)
    for run in range(2):
        at = slice(run * SLOTS, (run + 1) * SLOTS)
        weight = jnp.dot(coef_big[:, at], match[at], preferred_element_type=F32) + jnp.dot(
            coef_rest[:, at], match[at], preferred_element_type=F32
        )
        box = lax.broadcasted_iota(jnp.int32, weight.shape, 1)
        weight = jnp.where(box == parent[run * RUN], -jnp.maximum(weight, NO_WEIGHT), weight)
        for half in range(2):
            for side in range(2):
                wide[pl.ds(4 + half * 4 + run * 2 + side, DEVS, stride=ROWS), :] = weight[
                    half * DEVS : (half + 1) * DEVS, side * DEVS : (side + 1) * DEVS
                ]
    for k in range(CHUNKS // 2, CHUNKS):
        total[...] = total[...] + rays(k)
    for half in range(2):
        for run in range(2):
            wide[pl.ds(2 * half + run, DEVS, stride=ROWS), :] = total[
                half * DEVS : (half + 1) * DEVS, run * TIME : (run + 1) * TIME
            ]
    for edge, leaf in enumerate((0, 2 * RUN - 1)):
        for part in range(2):
            wide[pl.ds(12 + 2 * edge + part, DEVS, stride=ROWS), :] = cur[
                leaf, part * DEVS : (part + 1) * DEVS
            ].astype(F32)
    sent[...] = wide[...].astype(BF16)


def around(links, cur, leaf, at):
    def linked(run, side):
        value = cur[run, at + 2 * side - 1]
        return value * links[run * RUN + leaf, side].astype(F32).astype(BF16)

    own = jnp.concatenate([cur[run, at] for run in range(2)], axis=1)
    return [own] + [jnp.concatenate([linked(run, side) for run in range(2)], axis=1) for side in range(2)]


def near(links, cur_hbm, blocks_hbm, out_hbm, cur, blocks, stage, in_sems, blocks_sem, out_sems):
    steps = EARLY // STEP

    def fetch(k, run):
        first = 0 if k == 0 else 2 + k * STEP
        count = 2 + (k + 1) * STEP - first
        return pltpu.make_async_copy(
            cur_hbm.at[pl.ds(run * RUN + EDGE - 1 + first, count)],
            cur.at[run, pl.ds(first, count)],
            in_sems.at[run, k],
        )

    def store(k, run):
        return pltpu.make_async_copy(
            stage.at[run, pl.ds(k * STEP, STEP)], out_hbm.at[run, pl.ds(k * STEP, STEP)], out_sems.at[run, k]
        )

    load = pltpu.make_async_copy(blocks_hbm, blocks, blocks_sem)
    load.start()
    for k in range(steps):
        for run in range(2):
            fetch(k, run).start()
    load.wait()
    left = jnp.concatenate([blocks[j] for j in range(3)], axis=1)
    for k in range(steps):
        for run in range(2):
            fetch(k, run).wait()
        for j in range(k * STEP, (k + 1) * STEP):
            right = jnp.concatenate(around(links, cur, EDGE + j, 1 + j), axis=0)
            done = jnp.dot(left, right, preferred_element_type=F32)
            for run in range(2):
                stage[run, j] = done[:, run * TIME : (run + 1) * TIME].astype(NEAR)
        for run in range(2):
            store(k, run).start()
    for k in range(steps):
        for run in range(2):
            store(k, run).wait()


def translate(got, kernel, out, wide, tall):
    wide[...] = got[...].astype(F32)
    source = lax.broadcasted_iota(jnp.int32, (DEVS, TIME), 0)
    for part in range(2):
        first = wide[pl.ds(12 + part, DEVS, stride=ROWS), :]
        last = wide[pl.ds(14 + part, DEVS, stride=ROWS), :]
        tall[pl.ds(4 + part, DEVS, stride=BACK), :] = jnp.where(source == 0, 0.0, pltpu.roll(last, 1, 0))
        tall[pl.ds(6 + part, DEVS, stride=BACK), :] = jnp.where(
            source == DEVS - 1, 0.0, pltpu.roll(first, DEVS - 1, 0)
        )
    lag = jnp.broadcast_to(kernel[...], (TIME, TIME))
    lag = pltpu.roll(lag, 0, 1, stride=1, stride_axis=0)
    row = lax.broadcasted_iota(jnp.int32, (TIME, TIME), 0)
    column = lax.broadcasted_iota(jnp.int32, (TIME, TIME), 1)
    lag_big, lag_rest = split(jnp.where(column >= row, lag, 0.0))
    far = []
    for half in range(2):
        weight = jnp.concatenate(
            [
                jnp.concatenate(
                    [wide[pl.ds(4 + half * 4 + run * 2 + side, DEVS, stride=ROWS), :] for side in range(2)], axis=1
                )
                for run in range(2)
            ],
            axis=0,
        )
        if half == 0:
            place = jnp.where(weight < 0.0, 1.0, 0.0).astype(BF16)
        weight = jnp.abs(weight)
        weight = jnp.where(weight > NO_WEIGHT, weight, 0.0).astype(BF16)
        weight = lax.dot_general(weight, place, (((1,), (1,)), ((), ())), preferred_element_type=F32)
        rays = jnp.concatenate(
            [wide[pl.ds(2 * half + run, DEVS, stride=ROWS), :] for run in range(2)], axis=0
        )
        far.append(jnp.dot(weight.astype(BF16), rays.astype(BF16), preferred_element_type=F32))
    big, rest = split(jnp.concatenate(far, axis=0))
    done = (
        jnp.dot(big, lag_big, preferred_element_type=F32)
        + jnp.dot(rest, lag_big, preferred_element_type=F32)
        + jnp.dot(big, lag_rest, preferred_element_type=F32)
    )
    for k in range(4):
        tall[pl.ds(k, DEVS, stride=BACK), :] = done[k * DEVS : (k + 1) * DEVS]
    out[...] = tall[...].astype(BF16)


def disaggregate(
    links, got, blocks_hbm, cur_hbm, near_hbm, dis_hbm, out_hbm,
    blocks, cur, early, dis, stage, tall, incoming, cur_sems, early_sems, side_sems, out_sems,
):
    late = [(k % 2 * (RUN - EDGE) + k // 2 * STEP) for k in range(2 * EDGE // STEP)]
    early_steps = [EDGE + k * STEP for k in range(EARLY // STEP)]
    order = []
    for k in range(max(len(late), len(early_steps))):
        order += [(k, late[k], True)] if k < len(late) else []
        order += [(k, early_steps[k], False)] if k < len(early_steps) else []

    def fetch(k, first, is_late):
        at = pl.ds(first, STEP)
        copies = [pltpu.make_async_copy(dis_hbm.at[at], dis.at[at], side_sems.at[first // STEP])]
        for run in range(2):
            if is_late:
                start, end = first - 1, first + STEP + 1
                start = max(start, 0) if run == 0 else start
                end = min(end, RUN) if run == 1 else end
                copies.append(
                    pltpu.make_async_copy(
                        cur_hbm.at[pl.ds(run * RUN + start, end - start)],
                        cur.at[k, run, pl.ds(start - first + 1, end - start)],
                        cur_sems.at[run, k],
                    )
                )
            else:
                part = pl.ds(k * STEP, STEP)
                copies.append(
                    pltpu.make_async_copy(near_hbm.at[run, part], early.at[run, part], early_sems.at[run, k])
                )
        return copies

    def store(first, run):
        at = pl.ds(run * RUN + first, STEP)
        return pltpu.make_async_copy(stage.at[at], out_hbm.at[at], out_sems.at[run, first // STEP])

    load = pltpu.make_async_copy(blocks_hbm, blocks, side_sems.at[RUN // STEP])
    load.start()
    for part in order:
        for copy in fetch(*part):
            copy.start()
    tall[...] = got[...].astype(F32)
    for part in range(2):
        rows = slice(part * DEVS, (part + 1) * DEVS)
        cur[late.index(0), 0, 0, rows] = tall[pl.ds(4 + part, DEVS, stride=BACK), :].astype(BF16)
        cur[late.index(RUN - STEP), 1, STEP + 1, rows] = tall[pl.ds(6 + part, DEVS, stride=BACK), :].astype(BF16)
    for half in range(2):
        for run in range(2):
            incoming[half * DEVS : (half + 1) * DEVS, run * TIME : (run + 1) * TIME] = tall[
                pl.ds(2 * half + run, DEVS, stride=BACK), :
            ].astype(BF16)
    load.wait()
    left = jnp.concatenate([blocks[j] for j in range(3)], axis=1)
    for part in order:
        for copy in fetch(*part):
            copy.wait()
        k, first, is_late = part
        for j in range(STEP):
            leaf = first + j
            if is_late:
                right = jnp.concatenate(around(links, cur.at[k], leaf, 1 + j) + [incoming[...]], axis=0)
                done = jnp.dot(jnp.concatenate([left, dis[leaf]], axis=1), right, preferred_element_type=F32)
            else:
                done = jnp.dot(dis[leaf], incoming[...], preferred_element_type=F32)
            for run in range(2):
                value = done[:, run * TIME : (run + 1) * TIME]
                if not is_late:
                    value = value + early[run, k * STEP + j].astype(F32)
                stage[run * RUN + leaf] = value.astype(BF16)
        for run in range(2):
            store(first, run).start()
    for part in order:
        for run in range(2):
            store(part[1], run).wait()


def per_device(
    currents,
    leaf_parent,
    near_links,
    near_blocks,
    aggregate_maps,
    far_boxes,
    far_counts,
    translate_coef,
    time_kernel,
    disaggregate_maps,
):
    leaves = 2 * RUN
    hbm = whole(pltpu.HBM)
    sent = pl.pallas_call(
        aggregate,
        out_shape=jax.ShapeDtypeStruct((DEVS * ROWS, TIME), BF16),
        in_specs=[hbm] * 6,
        out_specs=whole(),
        scratch_shapes=[
            pltpu.VMEM((leaves, UNK, TIME), BF16),
            pltpu.VMEM((RUN, UNK, UNK), BF16),
            pltpu.VMEM((2, SLOTS, UNK), F32),
            pltpu.VMEM(far_boxes.shape, jnp.int32),
            pltpu.SMEM(leaf_parent.shape, jnp.int32),
            pltpu.SMEM(far_counts.shape, jnp.int32),
            pltpu.VMEM((DEVS * ROWS, TIME), F32),
            pltpu.VMEM((UNK, UNK), F32),
            pltpu.SemaphoreType.DMA((3, CHUNKS)),
            pltpu.SemaphoreType.DMA((5,)),
        ],
        compiler_params=params(40),
        cost_estimate=pl.CostEstimate(flops=2 << 30, bytes_accessed=17 * MIB, transcendentals=0),
        name="aggregate",
    )(*in_hbm(leaf_parent, far_counts, far_boxes, translate_coef, currents, aggregate_maps))
    arrived = lax.all_to_all(sent.reshape(DEVS, ROWS, TIME), AXES, 0, 0, tiled=True)
    early = pl.pallas_call(
        near,
        out_shape=pltpu.HBM((2, EARLY, UNK, TIME), NEAR),
        in_specs=[whole(pltpu.SMEM)] + [hbm] * 2,
        out_specs=hbm,
        scratch_shapes=[
            pltpu.VMEM((2, EARLY + 2, UNK, TIME), BF16),
            pltpu.VMEM((3, UNK, UNK), BF16),
            pltpu.VMEM((2, EARLY, UNK, TIME), NEAR),
            pltpu.SemaphoreType.DMA((2, EARLY // STEP)),
            pltpu.SemaphoreType.DMA(()),
            pltpu.SemaphoreType.DMA((2, EARLY // STEP)),
        ],
        compiler_params=params(40),
        cost_estimate=pl.CostEstimate(flops=3 << 30, bytes_accessed=12 * MIB, transcendentals=0),
        name="near",
    )(near_links, *in_hbm(currents, near_blocks))
    arrived, early = lax.optimization_barrier((arrived, early))
    incoming = pl.pallas_call(
        translate,
        out_shape=jax.ShapeDtypeStruct((DEVS * BACK, TIME), BF16),
        in_specs=[whole(), whole()],
        out_specs=whole(),
        scratch_shapes=[pltpu.VMEM((DEVS * ROWS, TIME), F32), pltpu.VMEM((DEVS * BACK, TIME), F32)],
        compiler_params=params(12),
        cost_estimate=pl.CostEstimate(flops=1 << 28, bytes_accessed=MIB, transcendentals=0),
        name="translate",
    )(arrived.reshape(DEVS * ROWS, TIME), time_kernel.reshape(1, TIME))
    returned = lax.all_to_all(incoming.reshape(DEVS, BACK, TIME), AXES, 0, 0, tiled=True)
    return pl.pallas_call(
        disaggregate,
        out_shape=pltpu.HBM((leaves, UNK, TIME), BF16),
        in_specs=[whole(pltpu.SMEM)] + [whole()] + [hbm] * 4,
        out_specs=hbm,
        scratch_shapes=[
            pltpu.VMEM((3, UNK, UNK), BF16),
            pltpu.VMEM((2 * EDGE // STEP, 2, STEP + 2, UNK, TIME), BF16),
            pltpu.VMEM((2, EARLY, UNK, TIME), NEAR),
            pltpu.VMEM((RUN, UNK, UNK), BF16),
            pltpu.VMEM((leaves, UNK, TIME), BF16),
            pltpu.VMEM((DEVS * BACK, TIME), F32),
            pltpu.VMEM((UNK, UNK), BF16),
            pltpu.SemaphoreType.DMA((2, 2 * EDGE // STEP)),
            pltpu.SemaphoreType.DMA((2, EARLY // STEP)),
            pltpu.SemaphoreType.DMA((RUN // STEP + 1,)),
            pltpu.SemaphoreType.DMA((2, RUN // STEP)),
        ],
        compiler_params=params(50),
        cost_estimate=pl.CostEstimate(flops=5 << 30, bytes_accessed=28 * MIB, transcendentals=0),
        name="disaggregate",
    )(
        near_links,
        returned.reshape(DEVS * BACK, TIME),
        *in_hbm(near_blocks, currents, early, disaggregate_maps),
    )


def solution(mesh):
    in_specs = (
        P(AXES, None, None),
        P(AXES),
        P(AXES, None),
        P(),
        P(),
        P("box", None),
        P("box"),
        P("box", None, None),
        P(),
        P(),
    )
    return jax.shard_map(
        per_device, mesh=mesh, in_specs=in_specs, out_specs=P(AXES, None, None), check_vma=False
    )
```

```python
import jax
import jax.numpy as jnp
from jax import lax
from jax.experimental import pallas as pl
from jax.experimental.pallas import tpu as pltpu
from jax.sharding import PartitionSpec as P

AXES = ("box", "dir")
RUN = 64
SLOTS = 64
CHUNKS = 8
CHUNK = RUN // CHUNKS
EARLY = 32
EDGE = (RUN - EARLY) // 2
STEP = 8
AHEAD = 3
KEPT = (0, EDGE)
UNK = 256
TIME = 128
DEVS = 128
ROWS = 16
F32, BF16 = jnp.float32, jnp.bfloat16
BACK = 8
NO_WEIGHT = 2.0**-30
NEAR = BF16
MIB = 1 << 20


def whole(space=pltpu.VMEM):
    return pl.BlockSpec(memory_space=space)


def params(mib):
    return pltpu.CompilerParams(vmem_limit_bytes=mib * MIB)


def in_hbm(*arrays):
    return [pltpu.with_memory_space_constraint(array, pltpu.HBM) for array in arrays]


def split(value):
    big = value.astype(BF16)
    return big, (value - big.astype(F32)).astype(BF16)


def aggregate(
    parent_hbm, counts_hbm, boxes_hbm, coef_hbm, cur_hbm, agg_hbm, sent,
    cur, maps, coef, boxes, parent, counts, wide, total, sems, small_sems,
):
    small = [
        pltpu.make_async_copy(source, target, small_sems.at[k])
        for k, (source, target) in enumerate(
            ((parent_hbm, parent), (counts_hbm, counts), (boxes_hbm, boxes))
        )
    ]
    for copy in small:
        copy.start()
    big = []
    for k in range(CHUNKS):
        part = pl.ds(k * CHUNK, CHUNK)
        second = pl.ds(RUN + k * CHUNK, CHUNK)
        big.append(
            (
                pltpu.make_async_copy(cur_hbm.at[part], cur.at[part], sems.at[0, k]),
                pltpu.make_async_copy(cur_hbm.at[second], cur.at[second], sems.at[1, k]),
                pltpu.make_async_copy(agg_hbm.at[part], maps.at[part], sems.at[2, k]),
            )
        )
    for copies in big[:AHEAD]:
        for copy in copies:
            copy.start()
    for copy in small:
        copy.wait()
    own = [lax.rem(parent[run * RUN], boxes.shape[0]) for run in range(2)]
    coef_copies = [
        pltpu.make_async_copy(coef_hbm.at[own[run]], coef.at[run], small_sems.at[3 + run]) for run in range(2)
    ]
    for copy in coef_copies:
        copy.start()

    def rays(k):
        for copy in big[k]:
            copy.wait()
        for copies in big[k + AHEAD : k + AHEAD + 1]:
            for copy in copies:
                copy.start()
        left = jnp.concatenate([maps[k * CHUNK + i] for i in range(CHUNK)], axis=1)
        right = jnp.concatenate(
            [cur[pl.ds(run * RUN + k * CHUNK, CHUNK)].reshape(CHUNK * UNK, TIME) for run in range(2)], axis=1
        )
        return jnp.dot(left, right, preferred_element_type=F32)

    total[...] = rays(0)
    for k in range(1, CHUNKS // 2):
        total[...] = total[...] + rays(k)
    for copy in coef_copies:
        copy.wait()
    row = lax.broadcasted_iota(jnp.int32, (2 * SLOTS, UNK), 0)
    used = row < jnp.where(row < SLOTS, counts[own[0]], SLOTS + counts[own[1]])
    turned = jnp.where(used, coef[...].reshape(2 * SLOTS, UNK), 0.0).T
    listed = jnp.concatenate([boxes[pl.ds(own[run], 1), :] for run in range(2)], axis=1)
    listed = jnp.broadcast_to(listed.astype(F32), (2 * SLOTS, 2 * SLOTS)).T[:, :1]
    lane = lax.broadcasted_iota(jnp.int32, (2 * SLOTS, 2 * DEVS), 1).astype(F32)
    match = jnp.where(listed == lane, 1.0, 0.0).astype(BF16)
    coef_big, coef_rest = split(turned)
    for run in range(2):
        at = slice(run * SLOTS, (run + 1) * SLOTS)
        weight = jnp.dot(coef_big[:, at], match[at], preferred_element_type=F32) + jnp.dot(
            coef_rest[:, at], match[at], preferred_element_type=F32
        )
        box = lax.broadcasted_iota(jnp.int32, weight.shape, 1)
        weight = jnp.where(box == parent[run * RUN], -jnp.maximum(weight, NO_WEIGHT), weight)
        for half in range(2):
            for side in range(2):
                wide[pl.ds(4 + half * 4 + run * 2 + side, DEVS, stride=ROWS), :] = weight[
                    half * DEVS : (half + 1) * DEVS, side * DEVS : (side + 1) * DEVS
                ]
    for k in range(CHUNKS // 2, CHUNKS):
        total[...] = total[...] + rays(k)
    for half in range(2):
        for run in range(2):
            wide[pl.ds(2 * half + run, DEVS, stride=ROWS), :] = total[
                half * DEVS : (half + 1) * DEVS, run * TIME : (run + 1) * TIME
            ]
    for edge, leaf in enumerate((0, 2 * RUN - 1)):
        for part in range(2):
            wide[pl.ds(12 + 2 * edge + part, DEVS, stride=ROWS), :] = cur[
                leaf, part * DEVS : (part + 1) * DEVS
            ].astype(F32)
    sent[...] = wide[...].astype(BF16)


def around(links, cur, leaf, at):
    def linked(run, side):
        value = cur[run, at + 2 * side - 1]
        return value * links[run * RUN + leaf, side].astype(F32).astype(BF16)

    own = jnp.concatenate([cur[run, at] for run in range(2)], axis=1)
    return [own] + [jnp.concatenate([linked(run, side) for run in range(2)], axis=1) for side in range(2)]


def near(
    links, cur_hbm, blocks_hbm, dis_hbm, out_hbm, kept, cur, blocks, stage, in_sems, blocks_sem, out_sems, kept_sems
):
    steps = EARLY // STEP

    def fetch(k, run):
        first = 0 if k == 0 else 2 + k * STEP
        count = 2 + (k + 1) * STEP - first
        return pltpu.make_async_copy(
            cur_hbm.at[pl.ds(run * RUN + EDGE - 1 + first, count)],
            cur.at[run, pl.ds(first, count)],
            in_sems.at[run, k],
        )

    def store(k, run):
        return pltpu.make_async_copy(
            stage.at[run, pl.ds(k * STEP, STEP)], out_hbm.at[run, pl.ds(k * STEP, STEP)], out_sems.at[run, k]
        )

    load = pltpu.make_async_copy(blocks_hbm, blocks, blocks_sem)
    load.start()
    for k in range(steps):
        for run in range(2):
            fetch(k, run).start()
    keep = [
        pltpu.make_async_copy(dis_hbm.at[pl.ds(first, STEP)], kept.at[pl.ds(k * STEP, STEP)], kept_sems.at[k])
        for k, first in enumerate(KEPT)
    ]
    for copy in keep:
        copy.start()
    load.wait()
    left = jnp.concatenate([blocks[j] for j in range(3)], axis=1)
    for k in range(steps):
        for run in range(2):
            fetch(k, run).wait()
        for j in range(k * STEP, (k + 1) * STEP):
            right = jnp.concatenate(around(links, cur, EDGE + j, 1 + j), axis=0)
            done = jnp.dot(left, right, preferred_element_type=F32)
            for run in range(2):
                stage[run, j] = done[:, run * TIME : (run + 1) * TIME].astype(NEAR)
        for run in range(2):
            store(k, run).start()
    for k in range(steps):
        for run in range(2):
            store(k, run).wait()
    for copy in keep:
        copy.wait()


def translate(got, kernel, out, wide, tall):
    wide[...] = got[...].astype(F32)
    source = lax.broadcasted_iota(jnp.int32, (DEVS, TIME), 0)
    for part in range(2):
        first = wide[pl.ds(12 + part, DEVS, stride=ROWS), :]
        last = wide[pl.ds(14 + part, DEVS, stride=ROWS), :]
        tall[pl.ds(4 + part, DEVS, stride=BACK), :] = jnp.where(source == 0, 0.0, pltpu.roll(last, 1, 0))
        tall[pl.ds(6 + part, DEVS, stride=BACK), :] = jnp.where(
            source == DEVS - 1, 0.0, pltpu.roll(first, DEVS - 1, 0)
        )
    lag = jnp.broadcast_to(kernel[...], (TIME, TIME))
    lag = pltpu.roll(lag, 0, 1, stride=1, stride_axis=0)
    row = lax.broadcasted_iota(jnp.int32, (TIME, TIME), 0)
    column = lax.broadcasted_iota(jnp.int32, (TIME, TIME), 1)
    lag_big, lag_rest = split(jnp.where(column >= row, lag, 0.0))
    far = []
    for half in range(2):
        weight = jnp.concatenate(
            [
                jnp.concatenate(
                    [wide[pl.ds(4 + half * 4 + run * 2 + side, DEVS, stride=ROWS), :] for side in range(2)], axis=1
                )
                for run in range(2)
            ],
            axis=0,
        )
        if half == 0:
            place = jnp.where(weight < 0.0, 1.0, 0.0).astype(BF16)
        weight = jnp.abs(weight)
        weight = jnp.where(weight > NO_WEIGHT, weight, 0.0).astype(BF16)
        weight = lax.dot_general(weight, place, (((1,), (1,)), ((), ())), preferred_element_type=F32)
        rays = jnp.concatenate(
            [wide[pl.ds(2 * half + run, DEVS, stride=ROWS), :] for run in range(2)], axis=0
        )
        far.append(jnp.dot(weight.astype(BF16), rays.astype(BF16), preferred_element_type=F32))
    big, rest = split(jnp.concatenate(far, axis=0))
    done = (
        jnp.dot(big, lag_big, preferred_element_type=F32)
        + jnp.dot(rest, lag_big, preferred_element_type=F32)
        + jnp.dot(big, lag_rest, preferred_element_type=F32)
    )
    for k in range(4):
        tall[pl.ds(k, DEVS, stride=BACK), :] = done[k * DEVS : (k + 1) * DEVS]
    out[...] = tall[...].astype(BF16)


def disaggregate(
    links, got, kept, blocks_hbm, cur_hbm, near_hbm, dis_hbm, out_hbm,
    blocks, cur, early, dis, stage, tall, incoming, cur_sems, early_sems, side_sems, out_sems,
):
    late = [(k % 2 * (RUN - EDGE) + k // 2 * STEP) for k in range(2 * EDGE // STEP)]
    early_steps = [EDGE + k * STEP for k in range(EARLY // STEP)]
    order = []
    for k in range(max(len(late), len(early_steps))):
        order += [(k, late[k], True)] if k < len(late) else []
        order += [(k, early_steps[k], False)] if k < len(early_steps) else []

    def fetch(k, first, is_late):
        at = pl.ds(first, STEP)
        copies = []
        if first not in KEPT:
            copies.append(pltpu.make_async_copy(dis_hbm.at[at], dis.at[at], side_sems.at[first // STEP]))
        for run in range(2):
            if is_late:
                start, end = first - 1, first + STEP + 1
                start = max(start, 0) if run == 0 else start
                end = min(end, RUN) if run == 1 else end
                copies.append(
                    pltpu.make_async_copy(
                        cur_hbm.at[pl.ds(run * RUN + start, end - start)],
                        cur.at[k, run, pl.ds(start - first + 1, end - start)],
                        cur_sems.at[run, k],
                    )
                )
            else:
                part = pl.ds(k * STEP, STEP)
                copies.append(
                    pltpu.make_async_copy(near_hbm.at[run, part], early.at[run, part], early_sems.at[run, k])
                )
        return copies

    def store(first, run):
        at = pl.ds(run * RUN + first, STEP)
        return pltpu.make_async_copy(stage.at[at], out_hbm.at[at], out_sems.at[run, first // STEP])

    load = pltpu.make_async_copy(blocks_hbm, blocks, side_sems.at[RUN // STEP])
    load.start()
    for part in order:
        for copy in fetch(*part):
            copy.start()
    tall[...] = got[...].astype(F32)
    for part in range(2):
        rows = slice(part * DEVS, (part + 1) * DEVS)
        cur[late.index(0), 0, 0, rows] = tall[pl.ds(4 + part, DEVS, stride=BACK), :].astype(BF16)
        cur[late.index(RUN - STEP), 1, STEP + 1, rows] = tall[pl.ds(6 + part, DEVS, stride=BACK), :].astype(BF16)
    for half in range(2):
        for run in range(2):
            incoming[half * DEVS : (half + 1) * DEVS, run * TIME : (run + 1) * TIME] = tall[
                pl.ds(2 * half + run, DEVS, stride=BACK), :
            ].astype(BF16)
    load.wait()
    left = jnp.concatenate([blocks[j] for j in range(3)], axis=1)
    for part in order:
        for copy in fetch(*part):
            copy.wait()
        k, first, is_late = part
        for j in range(STEP):
            leaf = first + j
            maps = kept[KEPT.index(first) * STEP + j] if first in KEPT else dis[leaf]
            if is_late:
                right = jnp.concatenate(around(links, cur.at[k], leaf, 1 + j) + [incoming[...]], axis=0)
                done = jnp.dot(jnp.concatenate([left, maps], axis=1), right, preferred_element_type=F32)
            else:
                done = jnp.dot(maps, incoming[...], preferred_element_type=F32)
            for run in range(2):
                value = done[:, run * TIME : (run + 1) * TIME]
                if not is_late:
                    value = value + early[run, k * STEP + j].astype(F32)
                stage[run * RUN + leaf] = value.astype(BF16)
        for run in range(2):
            store(first, run).start()
    for part in order:
        for run in range(2):
            store(part[1], run).wait()


def per_device(
    currents,
    leaf_parent,
    near_links,
    near_blocks,
    aggregate_maps,
    far_boxes,
    far_counts,
    translate_coef,
    time_kernel,
    disaggregate_maps,
):
    leaves = 2 * RUN
    hbm = whole(pltpu.HBM)
    sent = pl.pallas_call(
        aggregate,
        out_shape=jax.ShapeDtypeStruct((DEVS * ROWS, TIME), BF16),
        in_specs=[hbm] * 6,
        out_specs=whole(),
        scratch_shapes=[
            pltpu.VMEM((leaves, UNK, TIME), BF16),
            pltpu.VMEM((RUN, UNK, UNK), BF16),
            pltpu.VMEM((2, SLOTS, UNK), F32),
            pltpu.VMEM(far_boxes.shape, jnp.int32),
            pltpu.SMEM(leaf_parent.shape, jnp.int32),
            pltpu.SMEM(far_counts.shape, jnp.int32),
            pltpu.VMEM((DEVS * ROWS, TIME), F32),
            pltpu.VMEM((UNK, UNK), F32),
            pltpu.SemaphoreType.DMA((3, CHUNKS)),
            pltpu.SemaphoreType.DMA((5,)),
        ],
        compiler_params=params(40),
        cost_estimate=pl.CostEstimate(flops=2 << 30, bytes_accessed=17 * MIB, transcendentals=0),
        name="aggregate",
    )(*in_hbm(leaf_parent, far_counts, far_boxes, translate_coef, currents, aggregate_maps))
    arrived = lax.all_to_all(sent.reshape(DEVS, ROWS, TIME), AXES, 0, 0, tiled=True)
    early, kept = pl.pallas_call(
        near,
        out_shape=(
            pltpu.HBM((2, EARLY, UNK, TIME), NEAR),
            jax.ShapeDtypeStruct((len(KEPT) * STEP, UNK, UNK), BF16),
        ),
        in_specs=[whole(pltpu.SMEM)] + [hbm] * 3,
        out_specs=(hbm, whole()),
        scratch_shapes=[
            pltpu.VMEM((2, EARLY + 2, UNK, TIME), BF16),
            pltpu.VMEM((3, UNK, UNK), BF16),
            pltpu.VMEM((2, EARLY, UNK, TIME), NEAR),
            pltpu.SemaphoreType.DMA((2, EARLY // STEP)),
            pltpu.SemaphoreType.DMA(()),
            pltpu.SemaphoreType.DMA((2, EARLY // STEP)),
            pltpu.SemaphoreType.DMA((len(KEPT),)),
        ],
        compiler_params=params(40),
        cost_estimate=pl.CostEstimate(flops=3 << 30, bytes_accessed=12 * MIB, transcendentals=0),
        name="near",
    )(near_links, *in_hbm(currents, near_blocks, disaggregate_maps))
    arrived, early, kept = lax.optimization_barrier((arrived, early, kept))
    incoming = pl.pallas_call(
        translate,
        out_shape=jax.ShapeDtypeStruct((DEVS * BACK, TIME), BF16),
        in_specs=[whole(), whole()],
        out_specs=whole(),
        scratch_shapes=[pltpu.VMEM((DEVS * ROWS, TIME), F32), pltpu.VMEM((DEVS * BACK, TIME), F32)],
        compiler_params=params(12),
        cost_estimate=pl.CostEstimate(flops=1 << 28, bytes_accessed=MIB, transcendentals=0),
        name="translate",
    )(arrived.reshape(DEVS * ROWS, TIME), time_kernel.reshape(1, TIME))
    returned = lax.all_to_all(incoming.reshape(DEVS, BACK, TIME), AXES, 0, 0, tiled=True)
    return pl.pallas_call(
        disaggregate,
        out_shape=pltpu.HBM((leaves, UNK, TIME), BF16),
        in_specs=[whole(pltpu.SMEM)] + [whole()] * 2 + [hbm] * 4,
        out_specs=hbm,
        scratch_shapes=[
            pltpu.VMEM((3, UNK, UNK), BF16),
            pltpu.VMEM((2 * EDGE // STEP, 2, STEP + 2, UNK, TIME), BF16),
            pltpu.VMEM((2, EARLY, UNK, TIME), NEAR),
            pltpu.VMEM((RUN, UNK, UNK), BF16),
            pltpu.VMEM((leaves, UNK, TIME), BF16),
            pltpu.VMEM((DEVS * BACK, TIME), F32),
            pltpu.VMEM((UNK, UNK), BF16),
            pltpu.SemaphoreType.DMA((2, 2 * EDGE // STEP)),
            pltpu.SemaphoreType.DMA((2, EARLY // STEP)),
            pltpu.SemaphoreType.DMA((RUN // STEP + 1,)),
            pltpu.SemaphoreType.DMA((2, RUN // STEP)),
        ],
        compiler_params=params(50),
        cost_estimate=pl.CostEstimate(flops=5 << 30, bytes_accessed=28 * MIB, transcendentals=0),
        name="disaggregate",
    )(
        near_links,
        returned.reshape(DEVS * BACK, TIME),
        kept,
        *in_hbm(near_blocks, currents, early, disaggregate_maps),
    )


def solution(mesh):
    in_specs = (
        P(AXES, None, None),
        P(AXES),
        P(AXES, None),
        P(),
        P(),
        P("box", None),
        P("box"),
        P("box", None, None),
        P(),
        P(),
    )
    return jax.shard_map(
        per_device, mesh=mesh, in_specs=in_specs, out_specs=P(AXES, None, None), check_vma=False
    )
```

```python
import jax
import jax.numpy as jnp
from jax import lax
from jax.experimental import pallas as pl
from jax.experimental.pallas import tpu as pltpu
from jax.sharding import PartitionSpec as P

AXES = ("box", "dir")
RUN = 64
SLOTS = 64
CHUNKS = 8
CHUNK = RUN // CHUNKS
EARLY = 32
EDGE = (RUN - EARLY) // 2
STEP = 8
AHEAD = 3
WINDOW = 5
KEPT = (0, EDGE)
UNK = 256
TIME = 128
DEVS = 128
ROWS = 16
F32, BF16 = jnp.float32, jnp.bfloat16
BACK = 8
NO_WEIGHT = 2.0**-30
NEAR = BF16
MIB = 1 << 20


def whole(space=pltpu.VMEM):
    return pl.BlockSpec(memory_space=space)


def params(mib):
    return pltpu.CompilerParams(vmem_limit_bytes=mib * MIB)


def in_hbm(*arrays):
    return [pltpu.with_memory_space_constraint(array, pltpu.HBM) for array in arrays]


def split(value):
    big = value.astype(BF16)
    return big, (value - big.astype(F32)).astype(BF16)


def aggregate(
    parent_hbm, counts_hbm, boxes_hbm, coef_hbm, cur_hbm, agg_hbm, sent,
    cur, maps, coef, boxes, parent, counts, wide, total, sems, small_sems,
):
    small = [
        pltpu.make_async_copy(source, target, small_sems.at[k])
        for k, (source, target) in enumerate(
            ((parent_hbm, parent), (counts_hbm, counts), (boxes_hbm, boxes))
        )
    ]
    for copy in small:
        copy.start()
    big = []
    for k in range(CHUNKS):
        part = pl.ds(k * CHUNK, CHUNK)
        second = pl.ds(RUN + k * CHUNK, CHUNK)
        big.append(
            (
                pltpu.make_async_copy(cur_hbm.at[part], cur.at[part], sems.at[0, k]),
                pltpu.make_async_copy(cur_hbm.at[second], cur.at[second], sems.at[1, k]),
                pltpu.make_async_copy(agg_hbm.at[part], maps.at[part], sems.at[2, k]),
            )
        )
    for copies in big[:AHEAD]:
        for copy in copies:
            copy.start()
    for copy in small:
        copy.wait()
    own = [lax.rem(parent[run * RUN], boxes.shape[0]) for run in range(2)]
    coef_copies = [
        pltpu.make_async_copy(coef_hbm.at[own[run]], coef.at[run], small_sems.at[3 + run]) for run in range(2)
    ]
    for copy in coef_copies:
        copy.start()

    def rays(k):
        for copy in big[k]:
            copy.wait()
        for copies in big[k + AHEAD : k + AHEAD + 1]:
            for copy in copies:
                copy.start()
        left = jnp.concatenate([maps[k * CHUNK + i] for i in range(CHUNK)], axis=1)
        right = jnp.concatenate(
            [cur[pl.ds(run * RUN + k * CHUNK, CHUNK)].reshape(CHUNK * UNK, TIME) for run in range(2)], axis=1
        )
        return jnp.dot(left, right, preferred_element_type=F32)

    total[...] = rays(0)
    for k in range(1, CHUNKS // 2):
        total[...] = total[...] + rays(k)
    for copy in coef_copies:
        copy.wait()
    row = lax.broadcasted_iota(jnp.int32, (2 * SLOTS, UNK), 0)
    used = row < jnp.where(row < SLOTS, counts[own[0]], SLOTS + counts[own[1]])
    turned = jnp.where(used, coef[...].reshape(2 * SLOTS, UNK), 0.0).T
    listed = jnp.concatenate([boxes[pl.ds(own[run], 1), :] for run in range(2)], axis=1)
    listed = jnp.broadcast_to(listed.astype(F32), (2 * SLOTS, 2 * SLOTS)).T[:, :1]
    lane = lax.broadcasted_iota(jnp.int32, (2 * SLOTS, 2 * DEVS), 1).astype(F32)
    match = jnp.where(listed == lane, 1.0, 0.0).astype(BF16)
    coef_big, coef_rest = split(turned)
    for run in range(2):
        at = slice(run * SLOTS, (run + 1) * SLOTS)
        weight = jnp.dot(coef_big[:, at], match[at], preferred_element_type=F32) + jnp.dot(
            coef_rest[:, at], match[at], preferred_element_type=F32
        )
        box = lax.broadcasted_iota(jnp.int32, weight.shape, 1)
        weight = jnp.where(box == parent[run * RUN], -jnp.maximum(weight, NO_WEIGHT), weight)
        for half in range(2):
            for side in range(2):
                wide[pl.ds(4 + half * 4 + run * 2 + side, DEVS, stride=ROWS), :] = weight[
                    half * DEVS : (half + 1) * DEVS, side * DEVS : (side + 1) * DEVS
                ]
    for k in range(CHUNKS // 2, CHUNKS):
        total[...] = total[...] + rays(k)
    for half in range(2):
        for run in range(2):
            wide[pl.ds(2 * half + run, DEVS, stride=ROWS), :] = total[
                half * DEVS : (half + 1) * DEVS, run * TIME : (run + 1) * TIME
            ]
    for edge, leaf in enumerate((0, 2 * RUN - 1)):
        for part in range(2):
            wide[pl.ds(12 + 2 * edge + part, DEVS, stride=ROWS), :] = cur[
                leaf, part * DEVS : (part + 1) * DEVS
            ].astype(F32)
    sent[...] = wide[...].astype(BF16)


def around(links, cur, leaf, at):
    def linked(run, side):
        value = cur[run, at + 2 * side - 1]
        return value * links[run * RUN + leaf, side].astype(F32).astype(BF16)

    own = jnp.concatenate([cur[run, at] for run in range(2)], axis=1)
    return [own] + [jnp.concatenate([linked(run, side) for run in range(2)], axis=1) for side in range(2)]


def near(
    links, cur_hbm, blocks_hbm, dis_hbm, out_hbm, kept, cur, blocks, stage, in_sems, blocks_sem, out_sems, kept_sems
):
    steps = EARLY // STEP

    def fetch(k, run):
        first = 0 if k == 0 else 2 + k * STEP
        count = 2 + (k + 1) * STEP - first
        return pltpu.make_async_copy(
            cur_hbm.at[pl.ds(run * RUN + EDGE - 1 + first, count)],
            cur.at[run, pl.ds(first, count)],
            in_sems.at[run, k],
        )

    def store(k, run):
        return pltpu.make_async_copy(
            stage.at[run, pl.ds(k * STEP, STEP)], out_hbm.at[run, pl.ds(k * STEP, STEP)], out_sems.at[run, k]
        )

    load = pltpu.make_async_copy(blocks_hbm, blocks, blocks_sem)
    load.start()
    for k in range(steps):
        for run in range(2):
            fetch(k, run).start()
    keep = [
        pltpu.make_async_copy(dis_hbm.at[pl.ds(first, STEP)], kept.at[pl.ds(k * STEP, STEP)], kept_sems.at[k])
        for k, first in enumerate(KEPT)
    ]
    for copy in keep:
        copy.start()
    load.wait()
    left = jnp.concatenate([blocks[j] for j in range(3)], axis=1)
    for k in range(steps):
        for run in range(2):
            fetch(k, run).wait()
        for j in range(k * STEP, (k + 1) * STEP):
            right = jnp.concatenate(around(links, cur, EDGE + j, 1 + j), axis=0)
            done = jnp.dot(left, right, preferred_element_type=F32)
            for run in range(2):
                stage[run, j] = done[:, run * TIME : (run + 1) * TIME].astype(NEAR)
        for run in range(2):
            store(k, run).start()
    for k in range(steps):
        for run in range(2):
            store(k, run).wait()
    for copy in keep:
        copy.wait()


def translate(got, kernel, out, wide, tall):
    wide[...] = got[...].astype(F32)
    source = lax.broadcasted_iota(jnp.int32, (DEVS, TIME), 0)
    for part in range(2):
        first = wide[pl.ds(12 + part, DEVS, stride=ROWS), :]
        last = wide[pl.ds(14 + part, DEVS, stride=ROWS), :]
        tall[pl.ds(4 + part, DEVS, stride=BACK), :] = jnp.where(source == 0, 0.0, pltpu.roll(last, 1, 0))
        tall[pl.ds(6 + part, DEVS, stride=BACK), :] = jnp.where(
            source == DEVS - 1, 0.0, pltpu.roll(first, DEVS - 1, 0)
        )
    lag = jnp.broadcast_to(kernel[...], (TIME, TIME))
    lag = pltpu.roll(lag, 0, 1, stride=1, stride_axis=0)
    row = lax.broadcasted_iota(jnp.int32, (TIME, TIME), 0)
    column = lax.broadcasted_iota(jnp.int32, (TIME, TIME), 1)
    lag_big, lag_rest = split(jnp.where(column >= row, lag, 0.0))
    far = []
    for half in range(2):
        weight = jnp.concatenate(
            [
                jnp.concatenate(
                    [wide[pl.ds(4 + half * 4 + run * 2 + side, DEVS, stride=ROWS), :] for side in range(2)], axis=1
                )
                for run in range(2)
            ],
            axis=0,
        )
        if half == 0:
            place = jnp.where(weight < 0.0, 1.0, 0.0).astype(BF16)
        weight = jnp.abs(weight)
        weight = jnp.where(weight > NO_WEIGHT, weight, 0.0).astype(BF16)
        weight = lax.dot_general(weight, place, (((1,), (1,)), ((), ())), preferred_element_type=F32)
        rays = jnp.concatenate(
            [wide[pl.ds(2 * half + run, DEVS, stride=ROWS), :] for run in range(2)], axis=0
        )
        far.append(jnp.dot(weight.astype(BF16), rays.astype(BF16), preferred_element_type=F32))
    big, rest = split(jnp.concatenate(far, axis=0))
    done = (
        jnp.dot(big, lag_big, preferred_element_type=F32)
        + jnp.dot(rest, lag_big, preferred_element_type=F32)
        + jnp.dot(big, lag_rest, preferred_element_type=F32)
    )
    for k in range(4):
        tall[pl.ds(k, DEVS, stride=BACK), :] = done[k * DEVS : (k + 1) * DEVS]
    out[...] = tall[...].astype(BF16)


def disaggregate(
    links, got, kept, blocks_hbm, cur_hbm, near_hbm, dis_hbm, out_hbm,
    blocks, cur, early, dis, stage, tall, incoming, cur_sems, early_sems, side_sems, out_sems,
):
    late = [(k % 2 * (RUN - EDGE) + k // 2 * STEP) for k in range(2 * EDGE // STEP)]
    early_steps = [EDGE + k * STEP for k in range(EARLY // STEP)]
    order = []
    for k in range(max(len(late), len(early_steps))):
        order += [(k, late[k], True)] if k < len(late) else []
        order += [(k, early_steps[k], False)] if k < len(early_steps) else []

    def fetch(k, first, is_late):
        at = pl.ds(first, STEP)
        copies = []
        if first not in KEPT:
            copies.append(pltpu.make_async_copy(dis_hbm.at[at], dis.at[at], side_sems.at[first // STEP]))
        for run in range(2):
            if is_late:
                start, end = first - 1, first + STEP + 1
                start = max(start, 0) if run == 0 else start
                end = min(end, RUN) if run == 1 else end
                copies.append(
                    pltpu.make_async_copy(
                        cur_hbm.at[pl.ds(run * RUN + start, end - start)],
                        cur.at[k, run, pl.ds(start - first + 1, end - start)],
                        cur_sems.at[run, k],
                    )
                )
            else:
                part = pl.ds(k * STEP, STEP)
                copies.append(
                    pltpu.make_async_copy(near_hbm.at[run, part], early.at[run, part], early_sems.at[run, k])
                )
        return copies

    def store(first, run):
        at = pl.ds(run * RUN + first, STEP)
        return pltpu.make_async_copy(stage.at[at], out_hbm.at[at], out_sems.at[run, first // STEP])

    load = pltpu.make_async_copy(blocks_hbm, blocks, side_sems.at[RUN // STEP])
    load.start()
    for part in order[:WINDOW]:
        for copy in fetch(*part):
            copy.start()
    tall[...] = got[...].astype(F32)
    for part in range(2):
        rows = slice(part * DEVS, (part + 1) * DEVS)
        cur[late.index(0), 0, 0, rows] = tall[pl.ds(4 + part, DEVS, stride=BACK), :].astype(BF16)
        cur[late.index(RUN - STEP), 1, STEP + 1, rows] = tall[pl.ds(6 + part, DEVS, stride=BACK), :].astype(BF16)
    for half in range(2):
        for run in range(2):
            incoming[half * DEVS : (half + 1) * DEVS, run * TIME : (run + 1) * TIME] = tall[
                pl.ds(2 * half + run, DEVS, stride=BACK), :
            ].astype(BF16)
    load.wait()
    left = jnp.concatenate([blocks[j] for j in range(3)], axis=1)
    for n, part in enumerate(order):
        for copy in fetch(*part):
            copy.wait()
        for ahead in order[n + WINDOW : n + WINDOW + 1]:
            for copy in fetch(*ahead):
                copy.start()
        k, first, is_late = part
        for j in range(STEP):
            leaf = first + j
            maps = kept[KEPT.index(first) * STEP + j] if first in KEPT else dis[leaf]
            if is_late:
                right = jnp.concatenate(around(links, cur.at[k], leaf, 1 + j) + [incoming[...]], axis=0)
                done = jnp.dot(jnp.concatenate([left, maps], axis=1), right, preferred_element_type=F32)
            else:
                done = jnp.dot(maps, incoming[...], preferred_element_type=F32)
            for run in range(2):
                value = done[:, run * TIME : (run + 1) * TIME]
                if not is_late:
                    value = value + early[run, k * STEP + j].astype(F32)
                stage[run * RUN + leaf] = value.astype(BF16)
        for run in range(2):
            store(first, run).start()
    for part in order:
        for run in range(2):
            store(part[1], run).wait()


def per_device(
    currents,
    leaf_parent,
    near_links,
    near_blocks,
    aggregate_maps,
    far_boxes,
    far_counts,
    translate_coef,
    time_kernel,
    disaggregate_maps,
):
    leaves = 2 * RUN
    hbm = whole(pltpu.HBM)
    sent = pl.pallas_call(
        aggregate,
        out_shape=jax.ShapeDtypeStruct((DEVS * ROWS, TIME), BF16),
        in_specs=[hbm] * 6,
        out_specs=whole(),
        scratch_shapes=[
            pltpu.VMEM((leaves, UNK, TIME), BF16),
            pltpu.VMEM((RUN, UNK, UNK), BF16),
            pltpu.VMEM((2, SLOTS, UNK), F32),
            pltpu.VMEM(far_boxes.shape, jnp.int32),
            pltpu.SMEM(leaf_parent.shape, jnp.int32),
            pltpu.SMEM(far_counts.shape, jnp.int32),
            pltpu.VMEM((DEVS * ROWS, TIME), F32),
            pltpu.VMEM((UNK, UNK), F32),
            pltpu.SemaphoreType.DMA((3, CHUNKS)),
            pltpu.SemaphoreType.DMA((5,)),
        ],
        compiler_params=params(40),
        cost_estimate=pl.CostEstimate(flops=2 << 30, bytes_accessed=17 * MIB, transcendentals=0),
        name="aggregate",
    )(*in_hbm(leaf_parent, far_counts, far_boxes, translate_coef, currents, aggregate_maps))
    arrived = lax.all_to_all(sent.reshape(DEVS, ROWS, TIME), AXES, 0, 0, tiled=True)
    early, kept = pl.pallas_call(
        near,
        out_shape=(
            pltpu.HBM((2, EARLY, UNK, TIME), NEAR),
            jax.ShapeDtypeStruct((len(KEPT) * STEP, UNK, UNK), BF16),
        ),
        in_specs=[whole(pltpu.SMEM)] + [hbm] * 3,
        out_specs=(hbm, whole()),
        scratch_shapes=[
            pltpu.VMEM((2, EARLY + 2, UNK, TIME), BF16),
            pltpu.VMEM((3, UNK, UNK), BF16),
            pltpu.VMEM((2, EARLY, UNK, TIME), NEAR),
            pltpu.SemaphoreType.DMA((2, EARLY // STEP)),
            pltpu.SemaphoreType.DMA(()),
            pltpu.SemaphoreType.DMA((2, EARLY // STEP)),
            pltpu.SemaphoreType.DMA((len(KEPT),)),
        ],
        compiler_params=params(40),
        cost_estimate=pl.CostEstimate(flops=3 << 30, bytes_accessed=12 * MIB, transcendentals=0),
        name="near",
    )(near_links, *in_hbm(currents, near_blocks, disaggregate_maps))
    arrived, early, kept = lax.optimization_barrier((arrived, early, kept))
    incoming = pl.pallas_call(
        translate,
        out_shape=jax.ShapeDtypeStruct((DEVS * BACK, TIME), BF16),
        in_specs=[whole(), whole()],
        out_specs=whole(),
        scratch_shapes=[pltpu.VMEM((DEVS * ROWS, TIME), F32), pltpu.VMEM((DEVS * BACK, TIME), F32)],
        compiler_params=params(12),
        cost_estimate=pl.CostEstimate(flops=1 << 28, bytes_accessed=MIB, transcendentals=0),
        name="translate",
    )(arrived.reshape(DEVS * ROWS, TIME), time_kernel.reshape(1, TIME))
    returned = lax.all_to_all(incoming.reshape(DEVS, BACK, TIME), AXES, 0, 0, tiled=True)
    return pl.pallas_call(
        disaggregate,
        out_shape=pltpu.HBM((leaves, UNK, TIME), BF16),
        in_specs=[whole(pltpu.SMEM)] + [whole()] * 2 + [hbm] * 4,
        out_specs=hbm,
        scratch_shapes=[
            pltpu.VMEM((3, UNK, UNK), BF16),
            pltpu.VMEM((2 * EDGE // STEP, 2, STEP + 2, UNK, TIME), BF16),
            pltpu.VMEM((2, EARLY, UNK, TIME), NEAR),
            pltpu.VMEM((RUN, UNK, UNK), BF16),
            pltpu.VMEM((leaves, UNK, TIME), BF16),
            pltpu.VMEM((DEVS * BACK, TIME), F32),
            pltpu.VMEM((UNK, UNK), BF16),
            pltpu.SemaphoreType.DMA((2, 2 * EDGE // STEP)),
            pltpu.SemaphoreType.DMA((2, EARLY // STEP)),
            pltpu.SemaphoreType.DMA((RUN // STEP + 1,)),
            pltpu.SemaphoreType.DMA((2, RUN // STEP)),
        ],
        compiler_params=params(50),
        cost_estimate=pl.CostEstimate(flops=5 << 30, bytes_accessed=28 * MIB, transcendentals=0),
        name="disaggregate",
    )(
        near_links,
        returned.reshape(DEVS * BACK, TIME),
        kept,
        *in_hbm(near_blocks, currents, early, disaggregate_maps),
    )


def solution(mesh):
    in_specs = (
        P(AXES, None, None),
        P(AXES),
        P(AXES, None),
        P(),
        P(),
        P("box", None),
        P("box"),
        P("box", None, None),
        P(),
        P(),
    )
    return jax.shard_map(
        per_device, mesh=mesh, in_specs=in_specs, out_specs=P(AXES, None, None), check_vma=False
    )
```
